256 devices in a mesh: section: 32 (over z, x), dp: 8 (over y, core).
Axes of the slice: x: 4, y: 4, z: 8, core: 2. Of those that a mesh axis runs over, the one named last changes fastest.
Arguments:
- inputs: bfloat16 [1024, 4096], P('dp'), may hold values from -6 to 6
- gains: float32 [32, 4096], P('section'), may hold values from 0.1 to 1.9
- w_query: bfloat16 [32, 4096, 2048], P('section', 'dp'), may hold values from -0.09375 to 0.09375
- w_key: bfloat16 [32, 4096, 512], P('section', 'dp'), may hold values from -0.09375 to 0.09375
- w_value: bfloat16 [32, 4096, 512], P('section', 'dp'), may hold values from -0.09375 to 0.09375
- w_out: bfloat16 [32, 2048, 4096], P('section', 'dp'), may hold values from -0.125 to 0.125
Outputs:
- section_outputs: bfloat16 [32, 1024, 4096], P('section', 'dp')
The draws below stay inside these ranges and needn't reach their ends.
All inputs are finite; a program needn't handle non-finite values.
Results may differ from the reference program's by a relative error of at most 0.035.
Values may be sent and summed in bfloat16 or wider, within the bound.
A program may use at most 128 MiB of HBM per device.

```python
import jax
import jax.numpy as jnp
from jax import lax

D = 4096
HEADS = 16
KV = 4
HDIM = 128
SEQ = 128
TOKENS = 1024
N_SECTION = 32
N_DP = 8


def shard_levels(stream_key, shape, split, smallest, top_value):
    factor_of = 1.0
    for dim, blocks in split:
        heights = jax.random.uniform(jax.random.fold_in(jax.random.fold_in(stream_key, 6), dim), (blocks,), jnp.float32, smallest / len(split), top_value / len(split))
        factor_of = factor_of * jnp.repeat(jnp.exp(heights), shape[dim] // blocks).reshape((-1,) + (1,) * (len(shape) - 1 - dim))
    return factor_of


def bell_draw(rng, extent, spread, most, shards=(), held_as=jnp.bfloat16):
    values = spread * jax.random.normal(rng, extent, jnp.float32)
    if shards:
        values = values * shard_levels(rng, extent, shards, -0.22, 0.18)
    return jnp.clip(values, -most, most).astype(held_as)


def setup_inputs(seed: int = 0) -> dict:
    key_of = jax.random.split(jax.random.key(seed), 7)
    return {
        "inputs": bell_draw(key_of[0], (TOKENS, D), 1.0, 6.0, ((0, 8),)),
        "gains": jnp.clip(1.0 + 0.18 * jax.random.normal(key_of[1], (N_SECTION, D), jnp.float32), 0.1, 1.9),
        "w_query": bell_draw(key_of[2], (N_SECTION, D, HEADS * HDIM), D ** -0.5, 0.09375, ((0, 32), (1, 8))),
        "w_key": bell_draw(key_of[3], (N_SECTION, D, KV * HDIM), D ** -0.5, 0.09375, ((0, 32), (1, 8))),
        "w_value": bell_draw(key_of[4], (N_SECTION, D, KV * HDIM), D ** -0.5, 0.09375, ((0, 32), (1, 8))),
        "w_out": bell_draw(key_of[5], (N_SECTION, HEADS * HDIM, D), (HEADS * HDIM) ** -0.5, 0.125, ((0, 32), (1, 8))),
    }


def layer_apply(hidden, gain, w_query, w_key, w_value, w_out):
    rows = hidden.shape[0]
    groups = HEADS // KV
    xf = hidden.astype(jnp.float32)
    normed = (xf * lax.rsqrt(lax.optimization_barrier(jnp.mean(xf * xf, axis=-1, keepdims=True)) + 1e-05) * gain).astype(jnp.bfloat16)
    query = jnp.dot(normed, w_query, preferred_element_type=jnp.float32).astype(jnp.bfloat16)
    keys = jnp.dot(normed, w_key, preferred_element_type=jnp.float32).astype(jnp.bfloat16)
    values = jnp.dot(normed, w_value, preferred_element_type=jnp.float32).astype(jnp.bfloat16)
    qf = query.astype(jnp.float32).reshape(rows, KV, groups, HDIM)
    kf = keys.astype(jnp.float32).reshape(rows, KV, HDIM)
    vf = values.astype(jnp.float32).reshape(rows, KV, HDIM)
    scores = jnp.einsum('pkgd,skd->kgps', qf, kf) * (1.0 / HDIM ** 0.5)
    qpos = jnp.arange(rows, dtype=jnp.int32)
    allowed = qpos[None, :] <= qpos[:, None]
    scores = jnp.where(allowed, scores, -1e+30)
    peak = lax.optimization_barrier(jnp.max(scores, axis=-1, keepdims=True))
    expo = jnp.exp(scores - peak)
    probs = (expo / lax.optimization_barrier(jnp.sum(expo, axis=-1, keepdims=True))).astype(jnp.bfloat16)
    attended = jnp.einsum('kgps,skd->pkgd', probs.astype(jnp.float32), vf).astype(jnp.bfloat16)
    attended = attended.reshape(rows, HEADS * HDIM)
    return (xf + jnp.dot(attended, w_out, preferred_element_type=jnp.float32)).astype(jnp.bfloat16)

def reference(inputs, gains, w_query, w_key, w_value, w_out):
    sequences = inputs.reshape(N_DP, SEQ, D)

    def one_sequence(start):

        def step(hidden, params):
            gain, wq, wk, wv, wo = params
            result = layer_apply(hidden, gain, wq, wk, wv, wo)
            return (result, result)
        final, stacked = lax.scan(step, start, (gains, w_query, w_key, w_value, w_out))
        return stacked
    every = lax.map(one_sequence, sequences)
    return jnp.transpose(every, (1, 0, 2, 3)).reshape(N_SECTION, N_DP * SEQ, D)
```

```python
import functools

import jax
import jax.numpy as jnp
from jax import lax
from jax.experimental import pallas as pl
from jax.experimental.pallas import tpu as pltpu
from jax.sharding import PartitionSpec as P

MESH = pl.DeviceIdType.MESH
F32 = jnp.float32
BF16 = jnp.bfloat16

SECTIONS = 32
CHIPS = 4
D = 4096
HDIM = 128
SEQ = 128
GROUP = 4
ROWS = 16
PIECES = SEQ // ROWS
COUNT = 2 * PIECES
Q_W, K_W = 1024, 256
QKV_W = Q_W + 2 * K_W
HALF = D // 2
CHUNKS = 4
CW = HALF // CHUNKS
IN_ROWS, OUT_ROWS = 512, 256


def kernel(
    x_ref, gain_ref, wq_ref, wk_ref, wv_ref, wo_ref, out_ref,
    w_in, w_out, hbuf, stage, own_att, sib_att, keys, values, obuf,
    w_recv, w_send, f_send, h_recv, h_send, a_recv, a_send, o_recv, o_send, local,
):
    s = lax.axis_index("section")
    d = lax.axis_index("dp")
    y, c = d // 2, lax.rem(d, 2)
    other = 1 - c
    sibling = (s, y * 2 + other)

    def peer(step, core):
        return (s, lax.rem(y + step + CHIPS, CHIPS) * 2 + core)

    after = lax.rem(s + 1, SECTIONS)
    before = lax.rem(s + SECTIONS - 1, SECTIONS)

    barrier = pltpu.get_barrier_semaphore()
    greeted = [sibling]
    greeted += [peer(step, core) for step in (1, -1) for core in (0, 1)]
    greeted += [(sec, y * 2 + core) for sec in (after, before) for core in (0, 1)]
    for who in greeted:
        pl.semaphore_signal(barrier, inc=1, device_id=who, device_id_type=MESH)
    pl.semaphore_wait(barrier, len(greeted))

    def held(block, mat, core):
        if mat == 3:
            at = lax.rem(block + 8 - 4 * core, 8)
            return w_out.at[pl.ds(pl.multiple_of(at * OUT_ROWS, OUT_ROWS), OUT_ROWS), :]
        first, width = ((0, Q_W), (Q_W, K_W), (Q_W + K_W, K_W))[mat]
        return w_in.at[
            pl.ds(pl.multiple_of(block * IN_ROWS, IN_ROWS), IN_ROWS), pl.ds(first, width)
        ]

    def shard(mat, core):
        ref = (wq_ref, wk_ref, wv_ref, wo_ref)[mat]
        width = (Q_W, K_W, K_W, HALF)[mat]
        return ref.at[0, :, pl.ds(pl.multiple_of(core * width, width), width)]

    def direct(mat, slot, core, target):
        return pltpu.make_async_remote_copy(
            src_ref=shard(mat, core), dst_ref=held(d, mat, core),
            send_sem=w_send.at[mat, slot], recv_sem=w_recv.at[d, mat],
            device_id=target, device_id_type=MESH,
        )

    def forward(mat, slot, block, step):
        return pltpu.make_async_remote_copy(
            src_ref=held(block, mat, c), dst_ref=held(block, mat, c),
            send_sem=f_send.at[mat, slot], recv_sem=w_recv.at[block, mat],
            device_id=peer(step, c), device_id_type=MESH,
        )

    first_step = 2 * c - 1
    directs = []
    for mat in range(4):
        for slot, (step, core) in enumerate(
            ((first_step, c), (first_step, other), (-first_step, c), (-first_step, other))
        ):
            directs.append(direct(mat, slot, core, peer(step, core)))
        directs.append(direct(mat, 4, other, sibling))
    for copy in directs:
        copy.start()
    for mat in range(4):
        pltpu.make_async_copy(shard(mat, c), held(d, mat, c), w_recv.at[d, mat]).start()

    def chunk_cols(core, j):
        return pl.ds(pl.multiple_of(core * HALF + j * CW, CW), CW)

    @pl.when(s == 0)
    def _():
        def spread(p, carry):
            m = 2 * p + c
            copies = []
            for core in (0, 1):
                for j in range(CHUNKS):
                    src = x_ref.at[pl.ds(pl.multiple_of(p * ROWS, ROWS), ROWS), chunk_cols(core, j)]
                    dst = hbuf.at[m, :, chunk_cols(core, j)]
                    pltpu.make_async_copy(src, dst, h_recv.at[m, j, core]).start()
                    copy = pltpu.make_async_remote_copy(
                        src_ref=src, dst_ref=dst,
                        send_sem=h_send.at[0, j, core], recv_sem=h_recv.at[m, j, core],
                        device_id=sibling, device_id_type=MESH,
                    )
                    copy.start()
                    copies.append(copy)
            for copy in copies:
                copy.wait_send()
            return carry

        lax.fori_loop(0, PIECES, spread, 0)

    keys[...] = jnp.zeros_like(keys)
    values[...] = jnp.zeros_like(values)

    def arrived(ref, sem):
        pltpu.make_async_copy(ref, ref, sem).wait()

    from_up = lax.rem(y + 1, CHIPS) * 2
    from_down = lax.rem(y + CHIPS - 1, CHIPS) * 2 + 1
    forwards = []
    for mat in range(4):
        for slot, (block, step) in enumerate(((from_up, -1), (from_down, 1))):
            arrived(held(block, mat, c), w_recv.at[block, mat])
            copy = forward(mat, slot, block, step)
            copy.start()
            forwards.append(copy)
    rest = [
        d,
        y * 2 + other,
        from_up + 1,
        from_down - 1,
        lax.rem(y + 2, CHIPS) * 2,
        lax.rem(y + 2, CHIPS) * 2 + 1,
    ]
    for mat in range(4):
        for block in rest:
            arrived(held(block, mat, c), w_recv.at[block, mat])

    def to_next(m, j, core):
        return pltpu.make_async_remote_copy(
            src_ref=stage.at[m, :, pl.ds(j * CW, CW)], dst_ref=hbuf.at[m, :, chunk_cols(c, j)],
            send_sem=h_send.at[lax.rem(m, 2), j, core], recv_sem=h_recv.at[m, j, c],
            device_id=(after, y * 2 + core), device_id_type=MESH,
        )

    def to_sibling_att(m):
        return pltpu.make_async_remote_copy(
            src_ref=own_att.at[m], dst_ref=sib_att.at[m],
            send_sem=a_send.at[lax.rem(m, 2)], recv_sem=a_recv.at[m],
            device_id=sibling, device_id_type=MESH,
        )

    def out_rows(p):
        return pl.ds(pl.multiple_of(p * ROWS, ROWS), ROWS)

    def to_sibling_out(m):
        p = m // 2
        return pltpu.make_async_remote_copy(
            src_ref=stage.at[m],
            dst_ref=obuf.at[out_rows(p), pl.ds(pl.multiple_of(c * HALF, HALF), HALF)],
            send_sem=o_send.at[p], recv_sem=o_recv.at[p],
            device_id=sibling, device_id_type=MESH,
        )

    row_in_piece = lax.rem(
        lax.broadcasted_iota(jnp.int32, (GROUP * ROWS, SEQ), 0), jnp.int32(ROWS)
    )
    key_pos = lax.broadcasted_iota(jnp.int32, (GROUP * ROWS, SEQ), 1)

    def microbatch(m, carry):
        p, q = m // 2, lax.rem(m, 2)

        acc = jnp.zeros((ROWS, QKV_W), F32)
        squares = jnp.zeros((ROWS, 1), F32)
        for j in range(CHUNKS):
            for core in (0, 1):
                cols = pl.ds(core * HALF + j * CW, CW)
                arrived(hbuf.at[m, :, cols], h_recv.at[m, j, core])
                x = hbuf[m, :, cols].astype(F32)
                squares = squares + jnp.sum(x * x, axis=-1, keepdims=True)
                scaled = (x * gain_ref[:, cols]).astype(BF16)
                acc = acc + jnp.dot(scaled, w_in[cols, :], preferred_element_type=F32)
        acc = acc * lax.rsqrt(squares * (1.0 / D) + 1e-5)
        acc = acc.astype(BF16)
        rows = out_rows(p)
        keys[q, rows, :] = acc[:, Q_W : Q_W + K_W]
        values[q, rows, :] = acc[:, Q_W + K_W :]

        allowed = key_pos <= row_in_piece + p * ROWS
        for g in range(2):
            query = jnp.concatenate(
                [
                    acc[:, (g * GROUP + h) * HDIM : (g * GROUP + h + 1) * HDIM]
                    for h in range(GROUP)
                ],
                axis=0,
            )
            k = keys[q, :, g * HDIM : (g + 1) * HDIM]
            v = values[q, :, g * HDIM : (g + 1) * HDIM]
            scores = lax.dot_general(
                query, k, (((1,), (1,)), ((), ())), preferred_element_type=F32
            ) * (1.0 / HDIM**0.5)
            scores = jnp.where(allowed, scores, -1e30)
            expo = jnp.exp(scores - jnp.max(scores, axis=-1, keepdims=True))
            probs = (expo / jnp.sum(expo, axis=-1, keepdims=True)).astype(BF16)
            attended = jnp.dot(probs, v, preferred_element_type=F32).astype(BF16)
            for h in range(GROUP):
                at = (g * GROUP + h) * HDIM
                own_att[m, :, at : at + HDIM] = attended[h * ROWS : (h + 1) * ROWS, :]

        @pl.when(m >= 2)
        def _():
            to_sibling_att(m - 2).wait_send()

            @pl.when(s < SECTIONS - 1)
            def _():
                for j in range(CHUNKS):
                    for core in (0, 1):
                        to_next(m - 2, j, core).wait_send()

        to_sibling_att(m).start()

        own = jnp.dot(own_att[m], w_out[:Q_W, :], preferred_element_type=F32)
        arrived(sib_att.at[m], a_recv.at[m])
        sib = sib_att[m]
        for j in range(CHUNKS):
            cols = slice(j * CW, (j + 1) * CW)
            total = own[:, cols] + jnp.dot(sib, w_out[Q_W:, cols], preferred_element_type=F32)
            total = total + hbuf[m, :, chunk_cols(c, j)].astype(F32)
            stage[m, :, cols] = total.astype(BF16)

            @pl.when(s < SECTIONS - 1)
            def _():
                for core in (0, 1):
                    to_next(m, j, core).start()

        @pl.when(q == c)
        def _():
            obuf[rows, pl.ds(pl.multiple_of(c * HALF, HALF), HALF)] = stage[m]

        @pl.when(q != c)
        def _():
            to_sibling_out(m).start()

        return carry

    lax.fori_loop(0, COUNT, microbatch, 0)

    for m in (COUNT - 2, COUNT - 1):
        to_sibling_att(m).wait_send()

        @pl.when(s < SECTIONS - 1)
        def _():
            for j in range(CHUNKS):
                for core in (0, 1):
                    to_next(m, j, core).wait_send()

    def settle(p, carry):
        to_sibling_out(2 * p + other).wait_send()
        ref = obuf.at[out_rows(p), pl.ds(pl.multiple_of(other * HALF, HALF), HALF)]
        arrived(ref, o_recv.at[p])
        return carry

    lax.fori_loop(0, PIECES, settle, 0)
    result = pltpu.make_async_copy(obuf, out_ref.at[0], local)
    result.start()
    for copy in directs + forwards:
        copy.wait_send()
    result.wait()


def on_device(inputs, gains, w_query, w_key, w_value, w_out):
    anywhere = pl.BlockSpec(memory_space=pl.ANY)
    vmem = pl.BlockSpec(memory_space=pltpu.VMEM)
    dma = pltpu.SemaphoreType.DMA
    return pl.pallas_call(
        kernel,
        out_shape=jax.ShapeDtypeStruct((1, SEQ, D), BF16),
        in_specs=[anywhere, vmem, anywhere, anywhere, anywhere, anywhere],
        out_specs=anywhere,
        scratch_shapes=[
            pltpu.VMEM((D, QKV_W), BF16),
            pltpu.VMEM((2 * Q_W, HALF), BF16),
            pltpu.VMEM((COUNT, ROWS, D), BF16),
            pltpu.VMEM((COUNT, ROWS, HALF), BF16),
            pltpu.VMEM((COUNT, ROWS, Q_W), BF16),
            pltpu.VMEM((COUNT, ROWS, Q_W), BF16),
            pltpu.VMEM((2, SEQ, K_W), BF16),
            pltpu.VMEM((2, SEQ, K_W), BF16),
            pltpu.VMEM((SEQ, D), BF16),
            dma((8, 4)),
            dma((4, 5)),
            dma((4, 2)),
            dma((COUNT, CHUNKS, 2)),
            dma((2, CHUNKS, 2)),
            dma((COUNT,)),
            dma((2,)),
            dma((PIECES,)),
            dma((PIECES,)),
            dma(()),
        ],
        compiler_params=pltpu.CompilerParams(
            collective_id=0, has_side_effects=True, vmem_limit_bytes=56 * 2**20
        ),
    )(inputs, gains, w_query, w_key, w_value, w_out)


def solution(mesh):
    in_specs = (
        P("dp", None),
        P("section", None),
        P("section", "dp", None),
        P("section", "dp", None),
        P("section", "dp", None),
        P("section", "dp", None),
    )
    return jax.shard_map(
        on_device,
        mesh=mesh,
        in_specs=in_specs,
        out_specs=P("section", "dp", None),
        check_vma=False,
    )
```

```python
import functools

import jax
import jax.numpy as jnp
from jax import lax
from jax.experimental import pallas as pl
from jax.experimental.pallas import tpu as pltpu
from jax.sharding import PartitionSpec as P

MESH = pl.DeviceIdType.MESH
F32 = jnp.float32
BF16 = jnp.bfloat16

SECTIONS = 32
CHIPS = 4
D = 4096
HDIM = 128
SEQ = 128
GROUP = 4
G_W = GROUP * HDIM
ROWS = 16
PIECES = SEQ // ROWS
COUNT = 2 * PIECES
Q_W, K_W = 1024, 256
QKV_W = Q_W + 2 * K_W
HALF = D // 2
CHUNKS = 4
CW = HALF // CHUNKS
IN_ROWS, OUT_ROWS = 512, 256
PART = OUT_ROWS // 4
MATS = 3 + OUT_ROWS // PART
XS, ZS = 4, 8
DETOURS = 3


def kernel(
    x_ref, gain_ref, wq_ref, wk_ref, wv_ref, wo_ref, out_ref,
    w_in, w_out, lent, hbuf, stage, own_att, sib_att, keys, values, obuf,
    w_recv, w_send, f_send, l_recv, l_send, ld_send, lf_send, b_send, h_recv, h_send, r_send, a_recv, a_send, o_recv, o_send, local,
):
    s = lax.axis_index("section")
    d = lax.axis_index("dp")
    z, x_pos = s // XS, lax.rem(s, XS)
    y, c = d // 2, lax.rem(d, 2)
    other = 1 - c
    sibling = (s, y * 2 + other)

    def peer(step, core):
        return (s, lax.rem(y + step + CHIPS, CHIPS) * 2 + core)

    after = lax.rem(s + 1, SECTIONS)
    before = lax.rem(s + SECTIONS - 1, SECTIONS)

    barrier = pltpu.get_barrier_semaphore()
    greeted = [sibling]
    greeted += [peer(step, core) for step in (1, -1) for core in (0, 1)]
    above, below = lax.rem(s + XS, SECTIONS), lax.rem(s + SECTIONS - XS, SECTIONS)
    greeted += [(sec, y * 2 + core) for sec in (after, before, above, below) for core in (0, 1)]
    for who in greeted:
        pl.semaphore_signal(barrier, inc=1, device_id=who, device_id_type=MESH)
    pl.semaphore_wait(barrier, len(greeted))

    def part_rows(mat):
        return (mat - 3) * PART

    def held(block, mat, core):
        if not isinstance(mat, int) or mat >= 3:
            at = lax.rem(block + 8 - 4 * core, 8) * OUT_ROWS + part_rows(mat)
            return w_out.at[pl.ds(pl.multiple_of(at, PART), PART), :]
        first, width = ((0, Q_W), (Q_W, K_W), (Q_W + K_W, K_W))[mat]
        return w_in.at[
            pl.ds(pl.multiple_of(block * IN_ROWS, IN_ROWS), IN_ROWS), pl.ds(first, width)
        ]

    def shard(mat, core):
        if mat >= 3:
            cols = pl.ds(pl.multiple_of(core * HALF, HALF), HALF)
            return wo_ref.at[0, pl.ds(part_rows(mat), PART), cols]
        width = (Q_W, K_W, K_W)[mat]
        cols = pl.ds(pl.multiple_of(core * width, width), width)
        return (wq_ref, wk_ref, wv_ref)[mat].at[0, :, cols]

    def direct(mat, slot, core, target):
        return pltpu.make_async_remote_copy(
            src_ref=shard(mat, core), dst_ref=held(d, mat, core),
            send_sem=w_send.at[mat, slot], recv_sem=w_recv.at[d, mat],
            device_id=target, device_id_type=MESH,
        )

    def forward(mat, slot, block, step):
        return pltpu.make_async_remote_copy(
            src_ref=held(block, mat, c), dst_ref=held(block, mat, c),
            send_sem=f_send.at[mat, slot], recv_sem=w_recv.at[block, mat],
            device_id=peer(step, c), device_id_type=MESH,
        )

    def arrived(ref, sem):
        pltpu.make_async_copy(ref, ref, sem).wait()

    def detours(row):
        return jnp.where(row == 0, DETOURS, jnp.where(row < 4, DETOURS - 1, 0))

    mine = detours(z)
    served = jnp.where(z == ZS - 1, 0, z - 1)
    serves = jnp.where(jnp.logical_or(z == ZS - 1, z >= 2), detours(served), 0)
    helper = lax.rem(jnp.where(z == 0, ZS - 1, z + 1), ZS) * XS + x_pos
    client = lax.rem(served + ZS, ZS) * XS + x_pos

    def lend(k, core):
        return pltpu.make_async_remote_copy(
            src_ref=shard(MATS - 1 - k, core), dst_ref=lent.at[k, d],
            send_sem=l_send.at[k, core], recv_sem=l_recv.at[k, d],
            device_id=(helper, y * 2 + core), device_id_type=MESH,
        )

    def lent_on(k, block, sem, step):
        return pltpu.make_async_remote_copy(
            src_ref=lent.at[k, block], dst_ref=lent.at[k, block],
            send_sem=sem, recv_sem=l_recv.at[k, block],
            device_id=peer(step, c), device_id_type=MESH,
        )

    def give_back(k, slot, block):
        mat = MATS - 1 - k
        return pltpu.make_async_remote_copy(
            src_ref=lent.at[k, block], dst_ref=held(block, mat, c),
            send_sem=b_send.at[k, slot], recv_sem=w_recv.at[block, mat],
            device_id=(client, d), device_id_type=MESH,
        )

    from_up = lax.rem(y + 1, CHIPS) * 2
    from_down = lax.rem(y + CHIPS - 1, CHIPS) * 2 + 1
    across = lax.rem(y + 2, CHIPS) * 2
    passed = ((from_up, -1), (from_down, 1))

    def lent_directs(k):
        return [
            lent_on(k, y * 2 + core, ld_send.at[k, core, i], step)
            for core in (0, 1)
            for i, step in enumerate((1, -1))
        ]

    def lent_forwards(k):
        return [
            lent_on(k, block, lf_send.at[k, i], step) for i, (block, step) in enumerate(passed)
        ]

    others = (from_up, from_down, from_up + 1, from_down - 1, across, across + 1)

    def backs(k):
        return [give_back(k, slot, block) for slot, block in enumerate(others)]

    first_step = 2 * c - 1

    def directs(mat):
        return [
            direct(mat, slot, core, peer(step, core))
            for slot, (step, core) in enumerate(
                ((first_step, c), (first_step, other), (-first_step, c), (-first_step, other))
            )
        ]

    def forwards(mat):
        return [forward(mat, slot, block, step) for slot, (block, step) in enumerate(passed)]

    def in_ring(mat):
        return MATS - 1 - mat >= mine

    for k in range(DETOURS):

        @pl.when(k < mine)
        def _(k=k):
            for core in (0, 1):
                lend(k, core).start()

    for mat in range(MATS):
        direct(mat, 4, other, sibling).start()
        pltpu.make_async_copy(shard(mat, c), held(d, mat, c), w_recv.at[d, mat]).start()

    def start_inputs():
        for mat in range(3):
            for copy in directs(mat):
                copy.start()

    @pl.when(z < ZS - 1)
    def _():
        start_inputs()

    def serve(k, carry):
        for core in (0, 1):
            arrived(lent.at[k, y * 2 + core], l_recv.at[k, y * 2 + core])
        for copy in lent_directs(k):
            copy.start()
        onward = lent_forwards(k)
        for slot, block in enumerate(others):
            arrived(lent.at[k, block], l_recv.at[k, block])
            if slot < len(onward):
                onward[slot].start()
            give_back(k, slot, block).start()
        return carry

    lax.fori_loop(0, serves, serve, 0)

    @pl.when(z == ZS - 1)
    def _():
        start_inputs()

    for mat in range(3, MATS):

        @pl.when(in_ring(mat))
        def _(mat=mat):
            for copy in directs(mat):
                copy.start()

    def pass_on(mat):
        for copy, (block, _) in zip(forwards(mat), passed):
            arrived(held(block, mat, c), w_recv.at[block, mat])
            copy.start()

    for mat in range(MATS):
        if mat < 3:
            pass_on(mat)
        else:

            @pl.when(in_ring(mat))
            def _(mat=mat):
                pass_on(mat)

    def chunk_cols(core, j):
        return pl.ds(pl.multiple_of(core * HALF + j * CW, CW), CW)

    @pl.when(s == 0)
    def _():
        def spread(p, carry):
            m = 2 * p + c
            copies = []
            for core in (0, 1):
                for j in range(CHUNKS):
                    src = x_ref.at[pl.ds(pl.multiple_of(p * ROWS, ROWS), ROWS), chunk_cols(core, j)]
                    dst = hbuf.at[m, :, chunk_cols(core, j)]
                    pltpu.make_async_copy(src, dst, h_recv.at[m, j, core]).start()
                    copy = pltpu.make_async_remote_copy(
                        src_ref=src, dst_ref=dst,
                        send_sem=(r_send if core else h_send).at[m, j],
                        recv_sem=h_recv.at[m, j, core],
                        device_id=sibling, device_id_type=MESH,
                    )
                    copy.start()
                    copies.append(copy)
            for copy in copies:
                copy.wait_send()
            return carry

        lax.fori_loop(0, PIECES, spread, 0)

    keys[...] = jnp.zeros_like(keys)
    values[...] = jnp.zeros_like(values)

    for mat in range(MATS):
        for block in (d, y * 2 + other, *others[2:]):
            arrived(held(block, mat, c), w_recv.at[block, mat])
        if mat >= 3:

            @pl.when(jnp.logical_not(in_ring(mat)))
            def _(mat=mat):
                for block in others[:2]:
                    arrived(held(block, mat, c), w_recv.at[block, mat])

    def rows_of(p):
        return pl.ds(pl.multiple_of(p * ROWS, ROWS), ROWS)

    def to_next(m, j):
        return pltpu.make_async_remote_copy(
            src_ref=stage.at[lax.rem(m, 2), rows_of(m // 2), pl.ds(j * CW, CW)],
            dst_ref=hbuf.at[m, :, chunk_cols(c, j)],
            send_sem=h_send.at[m, j], recv_sem=h_recv.at[m, j, c],
            device_id=(after, d), device_id_type=MESH,
        )

    def to_sibling_rows(m, j):
        ref = hbuf.at[m, :, chunk_cols(c, j)]
        return pltpu.make_async_remote_copy(
            src_ref=ref, dst_ref=ref,
            send_sem=r_send.at[m, j], recv_sem=h_recv.at[m, j, c],
            device_id=sibling, device_id_type=MESH,
        )

    def to_sibling_att(m, g):
        return pltpu.make_async_remote_copy(
            src_ref=own_att.at[m, g], dst_ref=sib_att.at[m, g],
            send_sem=a_send.at[m, g], recv_sem=a_recv.at[m, g],
            device_id=sibling, device_id_type=MESH,
        )

    row_in_piece = lax.rem(
        lax.broadcasted_iota(jnp.int32, (GROUP * ROWS, SEQ), 0), jnp.int32(ROWS)
    )
    key_pos = lax.broadcasted_iota(jnp.int32, (GROUP * ROWS, SEQ), 1)

    def microbatch(first, last, m, carry):
        p, q = m // 2, lax.rem(m, 2)
        rows = rows_of(p)

        acc = jnp.zeros((ROWS, QKV_W), F32)
        squares = jnp.zeros((ROWS, 1), F32)
        for core in (c, other):
            for j in range(CHUNKS):
                cols = chunk_cols(core, j)
                arrived(hbuf.at[m, :, cols], h_recv.at[m, j, core])
                if core is c and not first:
                    to_sibling_rows(m, j).start()
                x = hbuf[m, :, cols].astype(F32)
                squares = squares + jnp.sum(x * x, axis=-1, keepdims=True)
                scaled = (x * gain_ref[:, cols]).astype(BF16)
                acc = acc + jnp.dot(scaled, w_in[cols, :], preferred_element_type=F32)
        acc = acc * lax.rsqrt(squares * (1.0 / D) + 1e-5)
        acc = acc.astype(BF16)
        keys[q, rows, :] = acc[:, Q_W : Q_W + K_W]
        values[q, rows, :] = acc[:, Q_W + K_W :]

        allowed = key_pos <= row_in_piece + p * ROWS
        expos = []
        for g in range(2):
            query = jnp.concatenate(
                [
                    acc[:, (g * GROUP + h) * HDIM : (g * GROUP + h + 1) * HDIM]
                    for h in range(GROUP)
                ],
                axis=0,
            )
            scores = lax.dot_general(
                query,
                keys[q, :, g * HDIM : (g + 1) * HDIM],
                (((1,), (1,)), ((), ())),
                preferred_element_type=F32,
            ) * (1.0 / HDIM**0.5)
            scores = jnp.where(allowed, scores, -1e30)
            expos.append(jnp.exp(scores - jnp.max(scores, axis=-1, keepdims=True)))
        sums = [jnp.sum(expo, axis=-1, keepdims=True) for expo in expos]
        for g in range(2):
            attended = jnp.dot(
                expos[g].astype(BF16),
                values[q, :, g * HDIM : (g + 1) * HDIM],
                preferred_element_type=F32,
            )
            attended = (attended / sums[g]).astype(BF16)
            for h in range(GROUP):
                own_att[m, g, :, h * HDIM : (h + 1) * HDIM] = attended[h * ROWS : (h + 1) * ROWS, :]
            to_sibling_att(m, g).start()

        total = hbuf[m, :, pl.ds(pl.multiple_of(c * HALF, HALF), HALF)].astype(F32)
        for g in range(2):
            total = total + jnp.dot(
                own_att[m, g], w_out[g * G_W : (g + 1) * G_W, :], preferred_element_type=F32
            )
        arrived(sib_att.at[m, 0], a_recv.at[m, 0])
        total = total + jnp.dot(
            sib_att[m, 0], w_out[2 * G_W : 3 * G_W, :], preferred_element_type=F32
        )
        arrived(sib_att.at[m, 1], a_recv.at[m, 1])
        sib = sib_att[m, 1]
        for j in range(CHUNKS):
            cols = slice(j * CW, (j + 1) * CW)
            part = total[:, cols] + jnp.dot(
                sib, w_out[3 * G_W :, cols], preferred_element_type=F32
            )
            stage[q, rows, cols] = part.astype(BF16)
            if not last:
                to_next(m, j).start()
        return carry

    def run(first, last):
        lax.fori_loop(0, COUNT, functools.partial(microbatch, first, last), 0)

        def settle(m, carry):
            for g in range(2):
                to_sibling_att(m, g).wait_send()
            for j in range(CHUNKS):
                if not last:
                    to_next(m, j).wait_send()
                if not first:
                    to_sibling_rows(m, j).wait_send()
            return carry

        lax.fori_loop(0, COUNT, settle, 0)

    swap = pltpu.make_async_remote_copy(
        src_ref=stage.at[other], dst_ref=obuf,
        send_sem=o_send, recv_sem=o_recv,
        device_id=sibling, device_id_type=MESH,
    )

    @pl.when(s == 0)
    def _():
        run(True, False)

    @pl.when(jnp.logical_and(s > 0, s < SECTIONS - 1))
    def _():
        run(False, False)

    @pl.when(s == SECTIONS - 1)
    def _():
        run(False, True)

    def result(src, core, sem):
        cols = pl.ds(pl.multiple_of(core * HALF, HALF), HALF)
        return pltpu.make_async_copy(src, out_ref.at[0, :, cols], sem)

    swap.start()
    result(stage.at[c], c, local.at[0]).start()
    swap.wait_recv()
    result(obuf, other, local.at[1]).start()
    for mat in range(MATS):
        direct(mat, 4, other, sibling).wait_send()

        @pl.when(in_ring(mat))
        def _(mat=mat):
            for copy in directs(mat) + forwards(mat):
                copy.wait_send()

    for k in range(DETOURS):

        @pl.when(k < mine)
        def _(k=k):
            for core in (0, 1):
                lend(k, core).wait_send()

    def served_all(k, carry):
        for copy in lent_directs(k) + lent_forwards(k) + backs(k):
            copy.wait_send()
        return carry

    lax.fori_loop(0, serves, served_all, 0)
    swap.wait_send()
    result(stage.at[c], c, local.at[0]).wait()
    result(obuf, other, local.at[1]).wait()


def on_device(inputs, gains, w_query, w_key, w_value, w_out):
    anywhere = pl.BlockSpec(memory_space=pl.ANY)
    vmem = pl.BlockSpec(memory_space=pltpu.VMEM)
    dma = pltpu.SemaphoreType.DMA
    return pl.pallas_call(
        kernel,
        out_shape=jax.ShapeDtypeStruct((1, SEQ, D), BF16),
        in_specs=[anywhere, vmem, anywhere, anywhere, anywhere, anywhere],
        out_specs=anywhere,
        scratch_shapes=[
            pltpu.VMEM((D, QKV_W), BF16),
            pltpu.VMEM((2 * Q_W, HALF), BF16),
            pltpu.VMEM((DETOURS, 8, PART, HALF), BF16),
            pltpu.VMEM((COUNT, ROWS, D), BF16),
            pltpu.VMEM((2, SEQ, HALF), BF16),
            pltpu.VMEM((COUNT, 2, ROWS, G_W), BF16),
            pltpu.VMEM((COUNT, 2, ROWS, G_W), BF16),
            pltpu.VMEM((2, SEQ, K_W), BF16),
            pltpu.VMEM((2, SEQ, K_W), BF16),
            pltpu.VMEM((SEQ, HALF), BF16),
            dma((8, MATS)),
            dma((MATS, 5)),
            dma((MATS, 2)),
            dma((DETOURS, 8)),
            dma((DETOURS, 2)),
            dma((DETOURS, 2, 2)),
            dma((DETOURS, 2)),
            dma((DETOURS, 6)),
            dma((COUNT, CHUNKS, 2)),
            dma((COUNT, CHUNKS)),
            dma((COUNT, CHUNKS)),
            dma((COUNT, 2)),
            dma((COUNT, 2)),
            dma(()),
            dma(()),
            dma((2,)),
        ],
        compiler_params=pltpu.CompilerParams(
            collective_id=0, has_side_effects=True, vmem_limit_bytes=56 * 2**20
        ),
    )(inputs, gains, w_query, w_key, w_value, w_out)


def solution(mesh):
    in_specs = (
        P("dp", None),
        P("section", None),
        P("section", "dp", None),
        P("section", "dp", None),
        P("section", "dp", None),
        P("section", "dp", None),
    )
    return jax.shard_map(
        on_device,
        mesh=mesh,
        in_specs=in_specs,
        out_specs=P("section", "dp", None),
        check_vma=False,
    )
```

```python
import functools

import jax
import jax.numpy as jnp
from jax import lax
from jax.experimental import pallas as pl
from jax.experimental.pallas import tpu as pltpu
from jax.sharding import PartitionSpec as P

MESH = pl.DeviceIdType.MESH
F32 = jnp.float32
BF16 = jnp.bfloat16

SECTIONS = 32
CHIPS = 4
D = 4096
HDIM = 128
SEQ = 128
GROUP = 4
G_W = GROUP * HDIM
ROWS = 16
PIECES = SEQ // ROWS
COUNT = 2 * PIECES
Q_W, K_W = 1024, 256
QKV_W = Q_W + 2 * K_W
HALF = D // 2
CHUNKS = 4
CW = HALF // CHUNKS
IN_ROWS, OUT_ROWS = 512, 256
PART = OUT_ROWS // 8
MATS = 3 + OUT_ROWS // PART
XS, ZS = 4, 8
FIRST_OUTER, FIRST_INNER = 5, 2
LATER = (6, 8, 7, 4)
DETOURS = max(FIRST_OUTER + FIRST_INNER, *LATER)


def kernel(
    x_ref, gain_ref, wq_ref, wk_ref, wv_ref, wo_ref, out_ref,
    w_in, w_out, lent, hbuf, stage, own_att, sib_att, keys, values, obuf,
    w_recv, w_send, f_send, l_recv, l_send, ld_send, lf_send, b_send, h_recv, h_send, r_send, a_recv, a_send, o_recv, o_send, local,
):
    s = lax.axis_index("section")
    d = lax.axis_index("dp")
    z, x_pos = s // XS, lax.rem(s, XS)
    y, c = d // 2, lax.rem(d, 2)
    other = 1 - c
    sibling = (s, y * 2 + other)

    def peer(step, core):
        return (s, lax.rem(y + step + CHIPS, CHIPS) * 2 + core)

    after = lax.rem(s + 1, SECTIONS)
    before = lax.rem(s + SECTIONS - 1, SECTIONS)

    barrier = pltpu.get_barrier_semaphore()
    greeted = [sibling]
    greeted += [peer(step, core) for step in (1, -1) for core in (0, 1)]
    above, below = lax.rem(s + XS, SECTIONS), lax.rem(s + SECTIONS - XS, SECTIONS)
    greeted += [(sec, y * 2 + core) for sec in (after, before, above, below) for core in (0, 1)]
    for who in greeted:
        pl.semaphore_signal(barrier, inc=1, device_id=who, device_id_type=MESH)
    pl.semaphore_wait(barrier, len(greeted))

    def part_rows(mat):
        return (mat - 3) * PART

    def held(block, mat, core):
        if not isinstance(mat, int) or mat >= 3:
            at = lax.rem(block + 8 - 4 * core, 8) * OUT_ROWS + part_rows(mat)
            return w_out.at[pl.ds(pl.multiple_of(at, PART), PART), :]
        first, width = ((0, Q_W), (Q_W, K_W), (Q_W + K_W, K_W))[mat]
        return w_in.at[
            pl.ds(pl.multiple_of(block * IN_ROWS, IN_ROWS), IN_ROWS), pl.ds(first, width)
        ]

    def shard(mat, core):
        if mat >= 3:
            cols = pl.ds(pl.multiple_of(core * HALF, HALF), HALF)
            return wo_ref.at[0, pl.ds(part_rows(mat), PART), cols]
        width = (Q_W, K_W, K_W)[mat]
        cols = pl.ds(pl.multiple_of(core * width, width), width)
        return (wq_ref, wk_ref, wv_ref)[mat].at[0, :, cols]

    def direct(mat, slot, core, target):
        return pltpu.make_async_remote_copy(
            src_ref=shard(mat, core), dst_ref=held(d, mat, core),
            send_sem=w_send.at[mat, slot], recv_sem=w_recv.at[d, mat],
            device_id=target, device_id_type=MESH,
        )

    def forward(mat, slot, block, step):
        return pltpu.make_async_remote_copy(
            src_ref=held(block, mat, c), dst_ref=held(block, mat, c),
            send_sem=f_send.at[mat, slot], recv_sem=w_recv.at[block, mat],
            device_id=peer(step, c), device_id_type=MESH,
        )

    def arrived(ref, sem):
        pltpu.make_async_copy(ref, ref, sem).wait()

    def by_row(values):
        total = 0
        for row, value in values.items():
            total = total + jnp.where(z == row, value, 0)
        return total

    mine = by_row({0: FIRST_OUTER + FIRST_INNER, **{r + 1: n for r, n in enumerate(LATER)}})
    serve_from = by_row({1: FIRST_OUTER})
    serve_to = by_row(
        {ZS - 1: FIRST_OUTER, 1: FIRST_OUTER + FIRST_INNER}
        | {r + 2: n for r, n in enumerate(LATER)}
    )
    client = jnp.where(z == ZS - 1, above, below)

    def helper(k):
        return jnp.where(jnp.logical_and(z == 0, k < FIRST_OUTER), below, above)

    def lend(k, core):
        return pltpu.make_async_remote_copy(
            src_ref=shard(MATS - 1 - k, core), dst_ref=lent.at[k, d],
            send_sem=l_send.at[k, core], recv_sem=l_recv.at[k, d],
            device_id=(helper(k), y * 2 + core), device_id_type=MESH,
        )

    def lent_on(k, block, sem, step):
        return pltpu.make_async_remote_copy(
            src_ref=lent.at[k, block], dst_ref=lent.at[k, block],
            send_sem=sem, recv_sem=l_recv.at[k, block],
            device_id=peer(step, c), device_id_type=MESH,
        )

    def give_back(k, slot, block):
        mat = MATS - 1 - k
        return pltpu.make_async_remote_copy(
            src_ref=lent.at[k, block], dst_ref=held(block, mat, c),
            send_sem=b_send.at[k, slot], recv_sem=w_recv.at[block, mat],
            device_id=(client, d), device_id_type=MESH,
        )

    from_up = lax.rem(y + 1, CHIPS) * 2
    from_down = lax.rem(y + CHIPS - 1, CHIPS) * 2 + 1
    across = lax.rem(y + 2, CHIPS) * 2
    passed = ((from_up, -1), (from_down, 1))

    def lent_directs(k):
        return [
            lent_on(k, y * 2 + core, ld_send.at[k, core, i], step)
            for core in (0, 1)
            for i, step in enumerate((1, -1))
        ]

    def lent_forwards(k):
        return [
            lent_on(k, block, lf_send.at[k, i], step) for i, (block, step) in enumerate(passed)
        ]

    others = (from_up, from_down, from_up + 1, from_down - 1, across, across + 1)

    def backs(k):
        return [give_back(k, slot, block) for slot, block in enumerate(others)]

    first_step = 2 * c - 1

    def directs(mat):
        return [
            direct(mat, slot, core, peer(step, core))
            for slot, (step, core) in enumerate(
                ((first_step, c), (first_step, other), (-first_step, c), (-first_step, other))
            )
        ]

    def forwards(mat):
        return [forward(mat, slot, block, step) for slot, (block, step) in enumerate(passed)]

    def in_ring(mat):
        return MATS - 1 - mat >= mine

    for k in range(DETOURS):

        @pl.when(k < mine)
        def _(k=k):
            for core in (0, 1):
                lend(k, core).start()

    for mat in range(MATS):
        direct(mat, 4, other, sibling).start()
        pltpu.make_async_copy(shard(mat, c), held(d, mat, c), w_recv.at[d, mat]).start()

    def start_all(mats):
        for mat in mats:
            for copy in directs(mat):
                copy.start()

    @pl.when(z < ZS - 1)
    def _():
        start_all((1, 2))

    def serve(k, carry):
        for core in (0, 1):
            arrived(lent.at[k, y * 2 + core], l_recv.at[k, y * 2 + core])
        for copy in lent_directs(k):
            copy.start()
        onward = lent_forwards(k)
        for slot, block in enumerate(others):
            arrived(lent.at[k, block], l_recv.at[k, block])
            if slot < len(onward):
                onward[slot].start()
            give_back(k, slot, block).start()
        return carry

    lax.fori_loop(serve_from, serve_to, serve, 0)

    @pl.when(z == ZS - 1)
    def _():
        start_all((1, 2))

    start_all((0,))

    for mat in range(3, MATS):

        @pl.when(in_ring(mat))
        def _(mat=mat):
            for copy in directs(mat):
                copy.start()

    def pass_on(mat):
        for copy, (block, _) in zip(forwards(mat), passed):
            arrived(held(block, mat, c), w_recv.at[block, mat])
            copy.start()

    for mat in range(MATS):
        if mat < 3:
            pass_on(mat)
        else:

            @pl.when(in_ring(mat))
            def _(mat=mat):
                pass_on(mat)

    def chunk_cols(core, j):
        return pl.ds(pl.multiple_of(core * HALF + j * CW, CW), CW)

    @pl.when(s == 0)
    def _():
        def spread(p, carry):
            m = 2 * p + c
            copies = []
            for core in (0, 1):
                for j in range(CHUNKS):
                    src = x_ref.at[pl.ds(pl.multiple_of(p * ROWS, ROWS), ROWS), chunk_cols(core, j)]
                    dst = hbuf.at[m, :, chunk_cols(core, j)]
                    pltpu.make_async_copy(src, dst, h_recv.at[m, j, core]).start()
                    copy = pltpu.make_async_remote_copy(
                        src_ref=src, dst_ref=dst,
                        send_sem=(r_send if core else h_send).at[m, j],
                        recv_sem=h_recv.at[m, j, core],
                        device_id=sibling, device_id_type=MESH,
                    )
                    copy.start()
                    copies.append(copy)
            for copy in copies:
                copy.wait_send()
            return carry

        lax.fori_loop(0, PIECES, spread, 0)

    keys[...] = jnp.zeros_like(keys)
    values[...] = jnp.zeros_like(values)

    for mat in range(MATS):
        for block in (d, y * 2 + other, *others[2:]):
            arrived(held(block, mat, c), w_recv.at[block, mat])
        if mat >= 3:

            @pl.when(jnp.logical_not(in_ring(mat)))
            def _(mat=mat):
                for block in others[:2]:
                    arrived(held(block, mat, c), w_recv.at[block, mat])

    def rows_of(p):
        return pl.ds(pl.multiple_of(p * ROWS, ROWS), ROWS)

    def to_next(m, j):
        return pltpu.make_async_remote_copy(
            src_ref=stage.at[lax.rem(m, 2), rows_of(m // 2), pl.ds(j * CW, CW)],
            dst_ref=hbuf.at[m, :, chunk_cols(c, j)],
            send_sem=h_send.at[m, j], recv_sem=h_recv.at[m, j, c],
            device_id=(after, d), device_id_type=MESH,
        )

    def to_sibling_rows(m, j):
        ref = hbuf.at[m, :, chunk_cols(c, j)]
        return pltpu.make_async_remote_copy(
            src_ref=ref, dst_ref=ref,
            send_sem=r_send.at[m, j], recv_sem=h_recv.at[m, j, c],
            device_id=sibling, device_id_type=MESH,
        )

    def to_sibling_att(m, g):
        return pltpu.make_async_remote_copy(
            src_ref=own_att.at[m, g], dst_ref=sib_att.at[m, g],
            send_sem=a_send.at[m, g], recv_sem=a_recv.at[m, g],
            device_id=sibling, device_id_type=MESH,
        )

    row_in_piece = lax.rem(
        lax.broadcasted_iota(jnp.int32, (GROUP * ROWS, SEQ), 0), jnp.int32(ROWS)
    )
    key_pos = lax.broadcasted_iota(jnp.int32, (GROUP * ROWS, SEQ), 1)

    def microbatch(first, last, m, carry):
        p, q = m // 2, lax.rem(m, 2)
        rows = rows_of(p)

        acc = jnp.zeros((ROWS, QKV_W), F32)
        squares = jnp.zeros((ROWS, 1), F32)
        for core in (c, other):
            for j in range(CHUNKS):
                cols = chunk_cols(core, j)
                arrived(hbuf.at[m, :, cols], h_recv.at[m, j, core])
                if core is c and not first:
                    to_sibling_rows(m, j).start()
                x = hbuf[m, :, cols].astype(F32)
                squares = squares + jnp.sum(x * x, axis=-1, keepdims=True)
                scaled = (x * gain_ref[:, cols]).astype(BF16)
                acc = acc + jnp.dot(scaled, w_in[cols, :], preferred_element_type=F32)
        acc = acc * lax.rsqrt(squares * (1.0 / D) + 1e-5)
        acc = acc.astype(BF16)
        keys[q, rows, :] = acc[:, Q_W : Q_W + K_W]
        values[q, rows, :] = acc[:, Q_W + K_W :]

        allowed = key_pos <= row_in_piece + p * ROWS
        expos = []
        for g in range(2):
            query = jnp.concatenate(
                [
                    acc[:, (g * GROUP + h) * HDIM : (g * GROUP + h + 1) * HDIM]
                    for h in range(GROUP)
                ],
                axis=0,
            )
            scores = lax.dot_general(
                query,
                keys[q, :, g * HDIM : (g + 1) * HDIM],
                (((1,), (1,)), ((), ())),
                preferred_element_type=F32,
            ) * (1.0 / HDIM**0.5)
            scores = jnp.where(allowed, scores, -1e30)
            expos.append(jnp.exp(scores - jnp.max(scores, axis=-1, keepdims=True)))
        sums = [jnp.sum(expo, axis=-1, keepdims=True) for expo in expos]
        for g in range(2):
            attended = jnp.dot(
                expos[g].astype(BF16),
                values[q, :, g * HDIM : (g + 1) * HDIM],
                preferred_element_type=F32,
            )
            attended = (attended / sums[g]).astype(BF16)
            for h in range(GROUP):
                own_att[m, g, :, h * HDIM : (h + 1) * HDIM] = attended[h * ROWS : (h + 1) * ROWS, :]
            to_sibling_att(m, g).start()

        total = hbuf[m, :, pl.ds(pl.multiple_of(c * HALF, HALF), HALF)].astype(F32)
        for g in range(2):
            total = total + jnp.dot(
                own_att[m, g], w_out[g * G_W : (g + 1) * G_W, :], preferred_element_type=F32
            )
        arrived(sib_att.at[m, 0], a_recv.at[m, 0])
        total = total + jnp.dot(
            sib_att[m, 0], w_out[2 * G_W : 3 * G_W, :], preferred_element_type=F32
        )
        arrived(sib_att.at[m, 1], a_recv.at[m, 1])
        sib = sib_att[m, 1]
        parts = []
        for j in range(CHUNKS + 1):
            if j < CHUNKS:
                cols = slice(j * CW, (j + 1) * CW)
                parts.append(
                    total[:, cols]
                    + jnp.dot(sib, w_out[3 * G_W :, cols], preferred_element_type=F32)
                )
            if j > 0:
                stage[q, rows, (j - 1) * CW : j * CW] = parts[j - 1].astype(BF16)
                if not last:
                    to_next(m, j - 1).start()
        return carry

    def run(first, last):
        lax.fori_loop(0, COUNT, functools.partial(microbatch, first, last), 0)

        def settle(m, carry):
            for g in range(2):
                to_sibling_att(m, g).wait_send()
            for j in range(CHUNKS):
                if not last:
                    to_next(m, j).wait_send()
                if not first:
                    to_sibling_rows(m, j).wait_send()
            return carry

        lax.fori_loop(0, COUNT, settle, 0)

    swap = pltpu.make_async_remote_copy(
        src_ref=stage.at[other], dst_ref=obuf,
        send_sem=o_send, recv_sem=o_recv,
        device_id=sibling, device_id_type=MESH,
    )

    @pl.when(s == 0)
    def _():
        run(True, False)

    @pl.when(jnp.logical_and(s > 0, s < SECTIONS - 1))
    def _():
        run(False, False)

    @pl.when(s == SECTIONS - 1)
    def _():
        run(False, True)

    def result(src, core, sem):
        cols = pl.ds(pl.multiple_of(core * HALF, HALF), HALF)
        return pltpu.make_async_copy(src, out_ref.at[0, :, cols], sem)

    swap.start()
    result(stage.at[c], c, local.at[0]).start()
    swap.wait_recv()
    result(obuf, other, local.at[1]).start()
    for mat in range(MATS):
        direct(mat, 4, other, sibling).wait_send()

        @pl.when(in_ring(mat))
        def _(mat=mat):
            for copy in directs(mat) + forwards(mat):
                copy.wait_send()

    for k in range(DETOURS):

        @pl.when(k < mine)
        def _(k=k):
            for core in (0, 1):
                lend(k, core).wait_send()

    def served_all(k, carry):
        for copy in lent_directs(k) + lent_forwards(k) + backs(k):
            copy.wait_send()
        return carry

    lax.fori_loop(serve_from, serve_to, served_all, 0)
    swap.wait_send()
    result(stage.at[c], c, local.at[0]).wait()
    result(obuf, other, local.at[1]).wait()


def on_device(inputs, gains, w_query, w_key, w_value, w_out):
    anywhere = pl.BlockSpec(memory_space=pl.ANY)
    vmem = pl.BlockSpec(memory_space=pltpu.VMEM)
    dma = pltpu.SemaphoreType.DMA
    return pl.pallas_call(
        kernel,
        out_shape=jax.ShapeDtypeStruct((1, SEQ, D), BF16),
        in_specs=[anywhere, vmem, anywhere, anywhere, anywhere, anywhere],
        out_specs=anywhere,
        scratch_shapes=[
            pltpu.VMEM((D, QKV_W), BF16),
            pltpu.VMEM((2 * Q_W, HALF), BF16),
            pltpu.VMEM((DETOURS, 8, PART, HALF), BF16),
            pltpu.VMEM((COUNT, ROWS, D), BF16),
            pltpu.VMEM((2, SEQ, HALF), BF16),
            pltpu.VMEM((COUNT, 2, ROWS, G_W), BF16),
            pltpu.VMEM((COUNT, 2, ROWS, G_W), BF16),
            pltpu.VMEM((2, SEQ, K_W), BF16),
            pltpu.VMEM((2, SEQ, K_W), BF16),
            pltpu.VMEM((SEQ, HALF), BF16),
            dma((8, MATS)),
            dma((MATS, 5)),
            dma((MATS, 2)),
            dma((DETOURS, 8)),
            dma((DETOURS, 2)),
            dma((DETOURS, 2, 2)),
            dma((DETOURS, 2)),
            dma((DETOURS, 6)),
            dma((COUNT, CHUNKS, 2)),
            dma((COUNT, CHUNKS)),
            dma((COUNT, CHUNKS)),
            dma((COUNT, 2)),
            dma((COUNT, 2)),
            dma(()),
            dma(()),
            dma((2,)),
        ],
        compiler_params=pltpu.CompilerParams(
            collective_id=0, has_side_effects=True, vmem_limit_bytes=56 * 2**20
        ),
    )(inputs, gains, w_query, w_key, w_value, w_out)


def solution(mesh):
    in_specs = (
        P("dp", None),
        P("section", None),
        P("section", "dp", None),
        P("section", "dp", None),
        P("section", "dp", None),
        P("section", "dp", None),
    )
    return jax.shard_map(
        on_device,
        mesh=mesh,
        in_specs=in_specs,
        out_specs=P("section", "dp", None),
        check_vma=False,
    )
```

```python
import functools

import jax
import jax.numpy as jnp
from jax import lax
from jax.experimental import pallas as pl
from jax.experimental.pallas import tpu as pltpu
from jax.sharding import PartitionSpec as P

MESH = pl.DeviceIdType.MESH
F32 = jnp.float32
BF16 = jnp.bfloat16

SECTIONS = 32
CHIPS = 4
D = 4096
HDIM = 128
SEQ = 128
GROUP = 4
G_W = GROUP * HDIM
ROWS = 16
PIECES = SEQ // ROWS
COUNT = 2 * PIECES
Q_W, K_W = 1024, 256
QKV_W = Q_W + 2 * K_W
HALF = D // 2
CHUNKS = 4
CW = HALF // CHUNKS
EARLY = 2
DEPTH = 128
IN_ROWS, OUT_ROWS = 512, 256
PART = OUT_ROWS // 8
Q_PARTS = 4
Q_ROWS = IN_ROWS // Q_PARTS
OUT_MAT = 2 + Q_PARTS
MATS = OUT_MAT + OUT_ROWS // PART
XS, ZS = 4, 8
FIRST_OUTER, FIRST_INNER = 5, 2
LATER = (6, 8, 7, 4)
SERVED_FIRST = 4
DETOURS = max(FIRST_OUTER + FIRST_INNER, *LATER)


def product(rows, weights):
    total = None
    for at in range(0, rows.shape[1], DEPTH):
        term = jnp.dot(
            rows[:, at : at + DEPTH], weights[at : at + DEPTH, :], preferred_element_type=F32
        )
        total = term if total is None else total + term
    return total


def kernel(
    x_ref, gain_ref, wq_ref, wk_ref, wv_ref, wo_ref, out_ref,
    w_in, w_out, lent, hbuf, stage, own_att, sib_att, keys, values, obuf,
    w_recv, w_send, f_send, l_recv, l_send, ld_send, lf_send, b_send, h_recv, h_send, r_send, a_recv, a_send, o_recv, o_send, local,
):
    s = lax.axis_index("section")
    d = lax.axis_index("dp")
    z, x_pos = s // XS, lax.rem(s, XS)
    y, c = d // 2, lax.rem(d, 2)
    other = 1 - c
    sibling = (s, y * 2 + other)

    def peer(step, core):
        return (s, lax.rem(y + step + CHIPS, CHIPS) * 2 + core)

    after = lax.rem(s + 1, SECTIONS)
    before = lax.rem(s + SECTIONS - 1, SECTIONS)

    barrier = pltpu.get_barrier_semaphore()
    greeted = [sibling]
    greeted += [peer(step, core) for step in (1, -1) for core in (0, 1)]
    above, below = lax.rem(s + XS, SECTIONS), lax.rem(s + SECTIONS - XS, SECTIONS)
    greeted += [(sec, y * 2 + core) for sec in (after, before, above, below) for core in (0, 1)]
    for who in greeted:
        pl.semaphore_signal(barrier, inc=1, device_id=who, device_id_type=MESH)
    pl.semaphore_wait(barrier, len(greeted))

    def out_part(block, mat, core):
        at = lax.rem(block + 8 - 4 * core, 8) * OUT_ROWS + (mat - OUT_MAT) * PART
        return w_out.at[pl.ds(pl.multiple_of(at, PART), PART), :]

    def query_part(block, mat):
        at = pl.multiple_of(block * IN_ROWS + (mat - 2) * Q_ROWS, Q_ROWS)
        return w_in.at[pl.ds(at, Q_ROWS), pl.ds(0, Q_W)]

    def held(block, mat, core):
        if mat < 2:
            rows = pl.ds(pl.multiple_of(block * IN_ROWS, IN_ROWS), IN_ROWS)
            return w_in.at[rows, pl.ds(Q_W + mat * K_W, K_W)]
        return query_part(block, mat) if mat < OUT_MAT else out_part(block, mat, core)

    def query_shard(mat, core):
        rows = pl.ds(pl.multiple_of((mat - 2) * Q_ROWS, Q_ROWS), Q_ROWS)
        return wq_ref.at[0, rows, pl.ds(pl.multiple_of(core * Q_W, Q_W), Q_W)]

    def shard(mat, core):
        if mat < 2:
            cols = pl.ds(pl.multiple_of(core * K_W, K_W), K_W)
            return (wk_ref, wv_ref)[mat].at[0, :, cols]
        if mat < OUT_MAT:
            return query_shard(mat, core)
        cols = pl.ds(pl.multiple_of(core * HALF, HALF), HALF)
        return wo_ref.at[0, pl.ds((mat - OUT_MAT) * PART, PART), cols]

    def direct(mat, slot, core, target):
        return pltpu.make_async_remote_copy(
            src_ref=shard(mat, core), dst_ref=held(d, mat, core),
            send_sem=w_send.at[mat, slot], recv_sem=w_recv.at[d, mat],
            device_id=target, device_id_type=MESH,
        )

    def forward(mat, slot, block, step):
        return pltpu.make_async_remote_copy(
            src_ref=held(block, mat, c), dst_ref=held(block, mat, c),
            send_sem=f_send.at[mat, slot], recv_sem=w_recv.at[block, mat],
            device_id=peer(step, c), device_id_type=MESH,
        )

    def arrived(ref, sem):
        pltpu.make_async_copy(ref, ref, sem).wait()

    def by_row(values):
        total = 0
        for row, value in values.items():
            total = total + jnp.where(z == row, value, 0)
        return total

    mine = by_row({0: FIRST_OUTER + FIRST_INNER, **{r + 1: n for r, n in enumerate(LATER)}})
    serve_from = by_row({1: FIRST_OUTER})
    serve_to = by_row(
        {ZS - 1: FIRST_OUTER, 1: FIRST_OUTER + FIRST_INNER}
        | {r + 2: n for r, n in enumerate(LATER)}
    )
    client = jnp.where(z == ZS - 1, above, below)

    def helper(k):
        return jnp.where(jnp.logical_and(z == 0, k < FIRST_OUTER), below, above)

    def lend(k, core):
        return pltpu.make_async_remote_copy(
            src_ref=shard(MATS - 1 - k, core), dst_ref=lent.at[k, d],
            send_sem=l_send.at[k, core], recv_sem=l_recv.at[k, d],
            device_id=(helper(k), y * 2 + core), device_id_type=MESH,
        )

    def lent_on(k, block, sem, step):
        return pltpu.make_async_remote_copy(
            src_ref=lent.at[k, block], dst_ref=lent.at[k, block],
            send_sem=sem, recv_sem=l_recv.at[k, block],
            device_id=peer(step, c), device_id_type=MESH,
        )

    def give_back(k, slot, block):
        mat = MATS - 1 - k
        return pltpu.make_async_remote_copy(
            src_ref=lent.at[k, block], dst_ref=out_part(block, mat, c),
            send_sem=b_send.at[k, slot], recv_sem=w_recv.at[block, mat],
            device_id=(client, d), device_id_type=MESH,
        )

    from_up = lax.rem(y + 1, CHIPS) * 2
    from_down = lax.rem(y + CHIPS - 1, CHIPS) * 2 + 1
    across = lax.rem(y + 2, CHIPS) * 2
    passed = ((from_up, -1), (from_down, 1))

    def lent_directs(k):
        return [
            lent_on(k, y * 2 + core, ld_send.at[k, core, i], step)
            for core in (0, 1)
            for i, step in enumerate((1, -1))
        ]

    def lent_forwards(k):
        return [
            lent_on(k, block, lf_send.at[k, i], step) for i, (block, step) in enumerate(passed)
        ]

    others = (from_up, from_down, from_up + 1, from_down - 1, across, across + 1)

    def backs(k):
        return [give_back(k, slot, block) for slot, block in enumerate(others)]

    first_step = 2 * c - 1

    ways = ((first_step, c), (first_step, other), (-first_step, c), (-first_step, other))

    def directs(mat):
        return [
            direct(mat, slot, core, peer(step, core)) for slot, (step, core) in enumerate(ways)
        ]

    def query_directs(mat):
        return [
            pltpu.make_async_remote_copy(
                src_ref=query_shard(mat, core), dst_ref=query_part(d, mat),
                send_sem=w_send.at[mat, slot], recv_sem=w_recv.at[d, mat],
                device_id=peer(step, core), device_id_type=MESH,
            )
            for slot, (step, core) in enumerate(ways)
        ]

    def forwards(mat):
        return [forward(mat, slot, block, step) for slot, (block, step) in enumerate(passed)]

    def in_ring(mat):
        return MATS - 1 - mat >= mine

    for k in range(DETOURS):

        @pl.when(k < mine)
        def _(k=k):
            for core in (0, 1):
                lend(k, core).start()

    def start_all(copies):
        for copy in copies:
            copy.start()

    @pl.when(z < ZS - 1)
    def _():
        start_all(directs(0) + directs(1))

    def serve(k, carry):
        for core in (0, 1):
            arrived(lent.at[k, y * 2 + core], l_recv.at[k, y * 2 + core])
        start_all(lent_directs(k))

        turn = k - serve_from - SERVED_FIRST

        @pl.when(jnp.logical_and(turn >= 0, turn < Q_PARTS))
        def _():
            start_all(query_directs(2 + turn))

        onward = lent_forwards(k)
        for slot, block in enumerate(others):
            arrived(lent.at[k, block], l_recv.at[k, block])
            if slot < len(onward):
                onward[slot].start()
            give_back(k, slot, block).start()
        return carry

    lax.fori_loop(serve_from, serve_to, serve, 0)

    @pl.when(z == ZS - 1)
    def _():
        start_all(directs(0) + directs(1))

    for mat in range(2, OUT_MAT):

        @pl.when(mat - 2 >= serve_to - serve_from - SERVED_FIRST)
        def _(mat=mat):
            start_all(query_directs(mat))

    for mat in range(OUT_MAT, MATS):

        @pl.when(in_ring(mat))
        def _(mat=mat):
            start_all(directs(mat))

    for mat in range(MATS):
        direct(mat, 4, other, sibling).start()
        pltpu.make_async_copy(shard(mat, c), held(d, mat, c), w_recv.at[d, mat]).start()

    def pass_on(mat):
        for copy, (block, _) in zip(forwards(mat), passed):
            arrived(held(block, mat, c), w_recv.at[block, mat])
            copy.start()

    for mat in range(MATS):
        if mat < OUT_MAT:
            pass_on(mat)
        else:

            @pl.when(in_ring(mat))
            def _(mat=mat):
                pass_on(mat)

    def chunk_cols(core, j):
        return pl.ds(pl.multiple_of(core * HALF + j * CW, CW), CW)

    @pl.when(s == 0)
    def _():
        def spread(p, carry):
            m = 2 * p + c
            copies = []
            for core in (0, 1):
                for j in range(CHUNKS):
                    src = x_ref.at[pl.ds(pl.multiple_of(p * ROWS, ROWS), ROWS), chunk_cols(core, j)]
                    dst = hbuf.at[m, :, chunk_cols(core, j)]
                    pltpu.make_async_copy(src, dst, h_recv.at[m, j, core]).start()
                    copy = pltpu.make_async_remote_copy(
                        src_ref=src, dst_ref=dst,
                        send_sem=(r_send if core else h_send).at[m, j],
                        recv_sem=h_recv.at[m, j, core],
                        device_id=sibling, device_id_type=MESH,
                    )
                    copy.start()
                    copies.append(copy)
            for copy in copies:
                copy.wait_send()
            return carry

        lax.fori_loop(0, PIECES, spread, 0)

    keys[...] = jnp.zeros_like(keys)
    values[...] = jnp.zeros_like(values)

    for mat in range(MATS):
        for block in (d, y * 2 + other, *others[2:]):
            arrived(held(block, mat, c), w_recv.at[block, mat])
        if mat >= OUT_MAT:

            @pl.when(jnp.logical_not(in_ring(mat)))
            def _(mat=mat):
                for block in others[:2]:
                    arrived(held(block, mat, c), w_recv.at[block, mat])

    def rows_of(p):
        return pl.ds(pl.multiple_of(p * ROWS, ROWS), ROWS)

    def to_next(m, j):
        return pltpu.make_async_remote_copy(
            src_ref=stage.at[lax.rem(m, 2), rows_of(m // 2), pl.ds(j * CW, CW)],
            dst_ref=hbuf.at[m, :, chunk_cols(c, j)],
            send_sem=h_send.at[m, j], recv_sem=h_recv.at[m, j, c],
            device_id=(after, d), device_id_type=MESH,
        )

    def to_sibling_rows(m, j):
        ref = hbuf.at[m, :, chunk_cols(c, j)]
        return pltpu.make_async_remote_copy(
            src_ref=ref, dst_ref=ref,
            send_sem=r_send.at[m, j], recv_sem=h_recv.at[m, j, c],
            device_id=sibling, device_id_type=MESH,
        )

    def to_sibling_att(m, g):
        return pltpu.make_async_remote_copy(
            src_ref=own_att.at[m, g], dst_ref=sib_att.at[m, g],
            send_sem=a_send.at[m, g], recv_sem=a_recv.at[m, g],
            device_id=sibling, device_id_type=MESH,
        )

    row_in_piece = lax.rem(
        lax.broadcasted_iota(jnp.int32, (GROUP * ROWS, SEQ), 0), jnp.int32(ROWS)
    )
    key_pos = lax.broadcasted_iota(jnp.int32, (GROUP * ROWS, SEQ), 1)

    def microbatch(first, last, m, carry):
        p, q = m // 2, lax.rem(m, 2)
        rows = rows_of(p)

        acc = jnp.zeros((ROWS, QKV_W), F32)
        squares = jnp.zeros((ROWS, HDIM), F32)
        for core in (c, other):
            for j in range(CHUNKS):
                cols = chunk_cols(core, j)
                arrived(hbuf.at[m, :, cols], h_recv.at[m, j, core])
                if core is c and not first:
                    to_sibling_rows(m, j).start()
                x = hbuf[m, :, cols].astype(F32)
                for at in range(0, CW, HDIM):
                    part = x[:, at : at + HDIM]
                    squares = squares + part * part
                scaled = (x * gain_ref[:, cols]).astype(BF16)
                acc = acc + product(scaled, w_in[cols, :])
        mean = jnp.sum(squares, axis=-1, keepdims=True) * (1.0 / D)
        acc = acc * lax.rsqrt(mean + 1e-5)
        acc = acc.astype(BF16)
        keys[q, rows, :] = acc[:, Q_W : Q_W + K_W]
        values[q, rows, :] = acc[:, Q_W + K_W :]

        allowed = key_pos <= row_in_piece + p * ROWS
        expos = []
        for g in range(2):
            query = jnp.concatenate(
                [
                    acc[:, (g * GROUP + h) * HDIM : (g * GROUP + h + 1) * HDIM]
                    for h in range(GROUP)
                ],
                axis=0,
            )
            scores = lax.dot_general(
                query,
                keys[q, :, g * HDIM : (g + 1) * HDIM],
                (((1,), (1,)), ((), ())),
                preferred_element_type=F32,
            ) * (1.0 / HDIM**0.5)
            scores = jnp.where(allowed, scores, -1e30)
            expos.append(jnp.exp(scores - jnp.max(scores, axis=-1, keepdims=True)))
        factors = [1.0 / jnp.sum(expo, axis=-1, keepdims=True) for expo in expos]
        owns = []
        for g in range(2):
            attended = jnp.dot(
                expos[g].astype(BF16),
                values[q, :, g * HDIM : (g + 1) * HDIM],
                preferred_element_type=F32,
            )
            attended = (attended * factors[g]).astype(BF16)
            attended = jnp.concatenate(
                [attended[h * ROWS : (h + 1) * ROWS, :] for h in range(GROUP)], axis=1
            )
            own_att[m, g] = attended
            owns.append(attended)
            to_sibling_att(m, g).start()

        total = hbuf[m, :, pl.ds(pl.multiple_of(c * HALF, HALF), HALF)].astype(F32)
        for g in range(2):
            total = total + product(owns[g], w_out[g * G_W : (g + 1) * G_W, :])

        def third(j):
            cols = slice(j * CW, (j + 1) * CW)
            return total[:, cols] + product(sib_0, w_out[2 * G_W : 3 * G_W, cols])

        arrived(sib_att.at[m, 0], a_recv.at[m, 0])
        sib_0 = sib_att[m, 0]
        parts = [third(j) for j in range(EARLY)]
        arrived(sib_att.at[m, 1], a_recv.at[m, 1])
        sib_1 = sib_att[m, 1]
        for j in range(CHUNKS + 1):
            if j < CHUNKS:
                if j >= EARLY:
                    parts.append(third(j))
                cols = slice(j * CW, (j + 1) * CW)
                parts[j] = parts[j] + product(sib_1, w_out[3 * G_W :, cols])
            if j > 0:
                stage[q, rows, (j - 1) * CW : j * CW] = parts[j - 1].astype(BF16)
                if not last:
                    to_next(m, j - 1).start()
        return carry

    def run(first, last):
        lax.fori_loop(0, COUNT, functools.partial(microbatch, first, last), 0)

        def settle(m, carry):
            for g in range(2):
                to_sibling_att(m, g).wait_send()
            for j in range(CHUNKS):
                if not last:
                    to_next(m, j).wait_send()
                if not first:
                    to_sibling_rows(m, j).wait_send()
            return carry

        lax.fori_loop(0, COUNT, settle, 0)

    swap = pltpu.make_async_remote_copy(
        src_ref=stage.at[other], dst_ref=obuf,
        send_sem=o_send, recv_sem=o_recv,
        device_id=sibling, device_id_type=MESH,
    )

    @pl.when(s == 0)
    def _():
        run(True, False)

    @pl.when(jnp.logical_and(s > 0, s < SECTIONS - 1))
    def _():
        run(False, False)

    @pl.when(s == SECTIONS - 1)
    def _():
        run(False, True)

    def result(src, core, sem):
        cols = pl.ds(pl.multiple_of(core * HALF, HALF), HALF)
        return pltpu.make_async_copy(src, out_ref.at[0, :, cols], sem)

    swap.start()
    result(stage.at[c], c, local.at[0]).start()
    swap.wait_recv()
    result(obuf, other, local.at[1]).start()
    for mat in range(MATS):
        direct(mat, 4, other, sibling).wait_send()

        @pl.when(in_ring(mat))
        def _(mat=mat):
            for copy in directs(mat) + forwards(mat):
                copy.wait_send()

    for k in range(DETOURS):

        @pl.when(k < mine)
        def _(k=k):
            for core in (0, 1):
                lend(k, core).wait_send()

    def served_all(k, carry):
        for copy in lent_directs(k) + lent_forwards(k) + backs(k):
            copy.wait_send()
        return carry

    lax.fori_loop(serve_from, serve_to, served_all, 0)
    swap.wait_send()
    result(stage.at[c], c, local.at[0]).wait()
    result(obuf, other, local.at[1]).wait()


def on_device(inputs, gains, w_query, w_key, w_value, w_out):
    anywhere = pl.BlockSpec(memory_space=pl.ANY)
    vmem = pl.BlockSpec(memory_space=pltpu.VMEM)
    dma = pltpu.SemaphoreType.DMA
    return pl.pallas_call(
        kernel,
        out_shape=jax.ShapeDtypeStruct((1, SEQ, D), BF16),
        in_specs=[anywhere, vmem, anywhere, anywhere, anywhere, anywhere],
        out_specs=anywhere,
        scratch_shapes=[
            pltpu.VMEM((D, QKV_W), BF16),
            pltpu.VMEM((2 * Q_W, HALF), BF16),
            pltpu.VMEM((DETOURS, 8, PART, HALF), BF16),
            pltpu.VMEM((COUNT, ROWS, D), BF16),
            pltpu.VMEM((2, SEQ, HALF), BF16),
            pltpu.VMEM((COUNT, 2, ROWS, G_W), BF16),
            pltpu.VMEM((COUNT, 2, ROWS, G_W), BF16),
            pltpu.VMEM((2, SEQ, K_W), BF16),
            pltpu.VMEM((2, SEQ, K_W), BF16),
            pltpu.VMEM((SEQ, HALF), BF16),
            dma((8, MATS)),
            dma((MATS, 5)),
            dma((MATS, 2)),
            dma((DETOURS, 8)),
            dma((DETOURS, 2)),
            dma((DETOURS, 2, 2)),
            dma((DETOURS, 2)),
            dma((DETOURS, 6)),
            dma((COUNT, CHUNKS, 2)),
            dma((COUNT, CHUNKS)),
            dma((COUNT, CHUNKS)),
            dma((COUNT, 2)),
            dma((COUNT, 2)),
            dma(()),
            dma(()),
            dma((2,)),
        ],
        compiler_params=pltpu.CompilerParams(
            collective_id=0, has_side_effects=True, vmem_limit_bytes=56 * 2**20
        ),
    )(inputs, gains, w_query, w_key, w_value, w_out)


def solution(mesh):
    in_specs = (
        P("dp", None),
        P("section", None),
        P("section", "dp", None),
        P("section", "dp", None),
        P("section", "dp", None),
        P("section", "dp", None),
    )
    return jax.shard_map(
        on_device,
        mesh=mesh,
        in_specs=in_specs,
        out_specs=P("section", "dp", None),
        check_vma=False,
    )
```

```python
import functools

import jax
import jax.numpy as jnp
from jax import lax
from jax.experimental import pallas as pl
from jax.experimental.pallas import tpu as pltpu
from jax.sharding import PartitionSpec as P

MESH = pl.DeviceIdType.MESH
F32 = jnp.float32
BF16 = jnp.bfloat16

SECTIONS = 32
CHIPS = 4
D = 4096
HDIM = 128
SEQ = 128
GROUP = 4
G_W = GROUP * HDIM
ROWS = 16
PIECES = SEQ // ROWS
COUNT = 2 * PIECES
Q_W, K_W = 1024, 256
QKV_W = Q_W + 2 * K_W
HALF = D // 2
CHUNKS = 4
CW = HALF // CHUNKS
EARLY = 2
DEPTH = 128
IN_ROWS, OUT_ROWS = 512, 256
PART = OUT_ROWS // 8
Q_PARTS = 4
Q_ROWS = IN_ROWS // Q_PARTS
OUT_MAT = 2 + Q_PARTS
MATS = OUT_MAT + OUT_ROWS // PART
XS, ZS = 4, 8
FIRST_OUTER, FIRST_INNER = 5, 2
LATER = (6, 8, 7, 4)
SERVED_FIRST = 4
DETOURS = max(FIRST_OUTER + FIRST_INNER, *LATER)


def product(rows, weights):
    total = None
    for at in range(0, rows.shape[1], DEPTH):
        term = jnp.dot(
            rows[:, at : at + DEPTH], weights[at : at + DEPTH, :], preferred_element_type=F32
        )
        total = term if total is None else total + term
    return total


def kernel(
    x_ref, gain_ref, wq_ref, wk_ref, wv_ref, wo_ref, out_ref,
    w_in, w_out, lent, hbuf, stage, own_att, sib_att, keys, values, obuf,
    w_recv, w_send, f_send, l_recv, l_send, ld_send, lf_send, b_send, h_recv, h_send, r_send, a_recv, a_send, o_recv, o_send, local,
):
    s = lax.axis_index("section")
    d = lax.axis_index("dp")
    z, x_pos = s // XS, lax.rem(s, XS)
    y, c = d // 2, lax.rem(d, 2)
    other = 1 - c
    sibling = (s, y * 2 + other)

    def peer(step, core):
        return (s, lax.rem(y + step + CHIPS, CHIPS) * 2 + core)

    after = lax.rem(s + 1, SECTIONS)
    before = lax.rem(s + SECTIONS - 1, SECTIONS)

    barrier = pltpu.get_barrier_semaphore()
    greeted = [sibling]
    greeted += [peer(step, core) for step in (1, -1) for core in (0, 1)]
    above, below = lax.rem(s + XS, SECTIONS), lax.rem(s + SECTIONS - XS, SECTIONS)
    greeted += [(sec, y * 2 + core) for sec in (after, before, above, below) for core in (0, 1)]
    for who in greeted:
        pl.semaphore_signal(barrier, inc=1, device_id=who, device_id_type=MESH)
    pl.semaphore_wait(barrier, len(greeted))

    def out_part(block, mat, core):
        at = lax.rem(block + 8 - 4 * core, 8) * OUT_ROWS + (mat - OUT_MAT) * PART
        return w_out.at[pl.ds(pl.multiple_of(at, PART), PART), :]

    def query_part(block, mat):
        at = pl.multiple_of(block * IN_ROWS + (mat - 2) * Q_ROWS, Q_ROWS)
        return w_in.at[pl.ds(at, Q_ROWS), pl.ds(0, Q_W)]

    def held(block, mat, core):
        if mat < 2:
            rows = pl.ds(pl.multiple_of(block * IN_ROWS, IN_ROWS), IN_ROWS)
            return w_in.at[rows, pl.ds(Q_W + mat * K_W, K_W)]
        return query_part(block, mat) if mat < OUT_MAT else out_part(block, mat, core)

    def query_shard(mat, core):
        rows = pl.ds(pl.multiple_of((mat - 2) * Q_ROWS, Q_ROWS), Q_ROWS)
        return wq_ref.at[0, rows, pl.ds(pl.multiple_of(core * Q_W, Q_W), Q_W)]

    def shard(mat, core):
        if mat < 2:
            cols = pl.ds(pl.multiple_of(core * K_W, K_W), K_W)
            return (wk_ref, wv_ref)[mat].at[0, :, cols]
        if mat < OUT_MAT:
            return query_shard(mat, core)
        cols = pl.ds(pl.multiple_of(core * HALF, HALF), HALF)
        return wo_ref.at[0, pl.ds((mat - OUT_MAT) * PART, PART), cols]

    def direct(mat, slot, core, target):
        return pltpu.make_async_remote_copy(
            src_ref=shard(mat, core), dst_ref=held(d, mat, core),
            send_sem=w_send.at[mat, slot], recv_sem=w_recv.at[d, mat],
            device_id=target, device_id_type=MESH,
        )

    def forward(mat, slot, block, step):
        return pltpu.make_async_remote_copy(
            src_ref=held(block, mat, c), dst_ref=held(block, mat, c),
            send_sem=f_send.at[mat, slot], recv_sem=w_recv.at[block, mat],
            device_id=peer(step, c), device_id_type=MESH,
        )

    def arrived(ref, sem):
        pltpu.make_async_copy(ref, ref, sem).wait()

    def by_row(values):
        total = 0
        for row, value in values.items():
            total = total + jnp.where(z == row, value, 0)
        return total

    mine = by_row({0: FIRST_OUTER + FIRST_INNER, **{r + 1: n for r, n in enumerate(LATER)}})
    serve_from = by_row({1: FIRST_OUTER})
    serve_to = by_row(
        {ZS - 1: FIRST_OUTER, 1: FIRST_OUTER + FIRST_INNER}
        | {r + 2: n for r, n in enumerate(LATER)}
    )
    client = jnp.where(z == ZS - 1, above, below)

    def helper(k):
        return jnp.where(jnp.logical_and(z == 0, k < FIRST_OUTER), below, above)

    def lend(k, core):
        return pltpu.make_async_remote_copy(
            src_ref=shard(MATS - 1 - k, core), dst_ref=lent.at[k, d],
            send_sem=l_send.at[k, core], recv_sem=l_recv.at[k, d],
            device_id=(helper(k), y * 2 + core), device_id_type=MESH,
        )

    def lent_on(k, block, sem, step):
        return pltpu.make_async_remote_copy(
            src_ref=lent.at[k, block], dst_ref=lent.at[k, block],
            send_sem=sem, recv_sem=l_recv.at[k, block],
            device_id=peer(step, c), device_id_type=MESH,
        )

    def give_back(k, slot, block):
        mat = MATS - 1 - k
        return pltpu.make_async_remote_copy(
            src_ref=lent.at[k, block], dst_ref=out_part(block, mat, c),
            send_sem=b_send.at[k, slot], recv_sem=w_recv.at[block, mat],
            device_id=(client, d), device_id_type=MESH,
        )

    from_up = lax.rem(y + 1, CHIPS) * 2
    from_down = lax.rem(y + CHIPS - 1, CHIPS) * 2 + 1
    across = lax.rem(y + 2, CHIPS) * 2
    passed = ((from_up, -1), (from_down, 1))

    def lent_directs(k):
        return [
            lent_on(k, y * 2 + core, ld_send.at[k, core, i], step)
            for core in (0, 1)
            for i, step in enumerate((1, -1))
        ]

    def lent_forwards(k):
        return [
            lent_on(k, block, lf_send.at[k, i], step) for i, (block, step) in enumerate(passed)
        ]

    others = (from_up, from_down, from_up + 1, from_down - 1, across, across + 1)

    def backs(k):
        return [give_back(k, slot, block) for slot, block in enumerate(others)]

    first_step = 2 * c - 1

    ways = ((first_step, c), (first_step, other), (-first_step, c), (-first_step, other))

    def directs(mat):
        return [
            direct(mat, slot, core, peer(step, core)) for slot, (step, core) in enumerate(ways)
        ]

    def query_directs(mat):
        return [
            pltpu.make_async_remote_copy(
                src_ref=query_shard(mat, core), dst_ref=query_part(d, mat),
                send_sem=w_send.at[mat, slot], recv_sem=w_recv.at[d, mat],
                device_id=peer(step, core), device_id_type=MESH,
            )
            for slot, (step, core) in enumerate(ways)
        ]

    def forwards(mat):
        return [forward(mat, slot, block, step) for slot, (block, step) in enumerate(passed)]

    def in_ring(mat):
        return MATS - 1 - mat >= mine

    for k in range(DETOURS):

        @pl.when(k < mine)
        def _(k=k):
            for core in (0, 1):
                lend(k, core).start()

    def start_all(copies):
        for copy in copies:
            copy.start()

    @pl.when(z < ZS - 1)
    def _():
        start_all(directs(0) + directs(1))

    def serve(k, carry):
        for core in (0, 1):
            arrived(lent.at[k, y * 2 + core], l_recv.at[k, y * 2 + core])
        start_all(lent_directs(k))

        turn = k - serve_from - SERVED_FIRST

        @pl.when(jnp.logical_and(turn >= 0, turn < Q_PARTS))
        def _():
            start_all(query_directs(2 + turn))

        onward = lent_forwards(k)
        for slot, block in enumerate(others):
            arrived(lent.at[k, block], l_recv.at[k, block])
            if slot < len(onward):
                onward[slot].start()
            give_back(k, slot, block).start()
        return carry

    lax.fori_loop(serve_from, serve_to, serve, 0)

    @pl.when(z == ZS - 1)
    def _():
        start_all(directs(0) + directs(1))

    for mat in range(2, OUT_MAT):

        @pl.when(mat - 2 >= serve_to - serve_from - SERVED_FIRST)
        def _(mat=mat):
            start_all(query_directs(mat))

    for mat in range(OUT_MAT, MATS):

        @pl.when(in_ring(mat))
        def _(mat=mat):
            start_all(directs(mat))

    for mat in range(MATS):
        direct(mat, 4, other, sibling).start()
        pltpu.make_async_copy(shard(mat, c), held(d, mat, c), w_recv.at[d, mat]).start()

    def pass_on(mat):
        for copy, (block, _) in zip(forwards(mat), passed):
            arrived(held(block, mat, c), w_recv.at[block, mat])
            copy.start()

    for mat in range(MATS):
        if mat < OUT_MAT:
            pass_on(mat)
        else:

            @pl.when(in_ring(mat))
            def _(mat=mat):
                pass_on(mat)

    def chunk_cols(core, j):
        return pl.ds(pl.multiple_of(core * HALF + j * CW, CW), CW)

    def spread(p, core, j, remote):
        m = 2 * p + c
        src = x_ref.at[pl.ds(pl.multiple_of(p * ROWS, ROWS), ROWS), chunk_cols(core, j)]
        dst = hbuf.at[m, :, chunk_cols(core, j)]
        if not remote:
            return pltpu.make_async_copy(src, dst, h_recv.at[m, j, core])
        return pltpu.make_async_remote_copy(
            src_ref=src, dst_ref=dst,
            send_sem=r_send.at[2 * p + core, j], recv_sem=h_recv.at[m, j, core],
            device_id=sibling, device_id_type=MESH,
        )

    @pl.when(s == 0)
    def _():
        def start_piece(p, carry):
            for core in (0, 1):
                for j in range(CHUNKS):
                    for remote in (False, True):
                        spread(p, core, j, remote).start()
            return carry

        lax.fori_loop(0, PIECES, start_piece, 0)

    keys[...] = jnp.zeros_like(keys)
    values[...] = jnp.zeros_like(values)

    for mat in range(MATS):
        for block in (d, y * 2 + other, *others[2:]):
            arrived(held(block, mat, c), w_recv.at[block, mat])
        if mat >= OUT_MAT:

            @pl.when(jnp.logical_not(in_ring(mat)))
            def _(mat=mat):
                for block in others[:2]:
                    arrived(held(block, mat, c), w_recv.at[block, mat])

    def rows_of(p):
        return pl.ds(pl.multiple_of(p * ROWS, ROWS), ROWS)

    def to_next(m, j):
        return pltpu.make_async_remote_copy(
            src_ref=stage.at[lax.rem(m, 2), rows_of(m // 2), pl.ds(j * CW, CW)],
            dst_ref=hbuf.at[m, :, chunk_cols(c, j)],
            send_sem=h_send.at[m, j], recv_sem=h_recv.at[m, j, c],
            device_id=(after, d), device_id_type=MESH,
        )

    def to_sibling_rows(m, j):
        ref = hbuf.at[m, :, chunk_cols(c, j)]
        return pltpu.make_async_remote_copy(
            src_ref=ref, dst_ref=ref,
            send_sem=r_send.at[m, j], recv_sem=h_recv.at[m, j, c],
            device_id=sibling, device_id_type=MESH,
        )

    def to_sibling_att(m, g):
        return pltpu.make_async_remote_copy(
            src_ref=own_att.at[m, g], dst_ref=sib_att.at[m, g],
            send_sem=a_send.at[m, g], recv_sem=a_recv.at[m, g],
            device_id=sibling, device_id_type=MESH,
        )

    row_in_piece = lax.rem(
        lax.broadcasted_iota(jnp.int32, (GROUP * ROWS, SEQ), 0), jnp.int32(ROWS)
    )
    key_pos = lax.broadcasted_iota(jnp.int32, (GROUP * ROWS, SEQ), 1)

    def microbatch(first, last, m, carry):
        p, q = m // 2, lax.rem(m, 2)
        rows = rows_of(p)

        acc = jnp.zeros((ROWS, QKV_W), F32)
        squares = jnp.zeros((ROWS, HDIM), F32)
        for core in (c, other):
            for j in range(CHUNKS):
                cols = chunk_cols(core, j)
                arrived(hbuf.at[m, :, cols], h_recv.at[m, j, core])
                if core is c and not first:
                    to_sibling_rows(m, j).start()
                x = hbuf[m, :, cols].astype(F32)
                for at in range(0, CW, HDIM):
                    part = x[:, at : at + HDIM]
                    squares = squares + part * part
                scaled = (x * gain_ref[:, cols]).astype(BF16)
                acc = acc + product(scaled, w_in[cols, :])
        mean = jnp.sum(squares, axis=-1, keepdims=True) * (1.0 / D)
        acc = acc * lax.rsqrt(mean + 1e-5)
        acc = acc.astype(BF16)
        keys[q, rows, :] = acc[:, Q_W : Q_W + K_W]
        values[q, rows, :] = acc[:, Q_W + K_W :]

        allowed = key_pos <= row_in_piece + p * ROWS
        expos = []
        for g in range(2):
            query = jnp.concatenate(
                [
                    acc[:, (g * GROUP + h) * HDIM : (g * GROUP + h + 1) * HDIM]
                    for h in range(GROUP)
                ],
                axis=0,
            )
            scores = lax.dot_general(
                query,
                keys[q, :, g * HDIM : (g + 1) * HDIM],
                (((1,), (1,)), ((), ())),
                preferred_element_type=F32,
            ) * (1.0 / HDIM**0.5)
            scores = jnp.where(allowed, scores, -1e30)
            expos.append(jnp.exp(scores - jnp.max(scores, axis=-1, keepdims=True)))
        factors = [1.0 / jnp.sum(expo, axis=-1, keepdims=True) for expo in expos]
        owns = []
        for g in range(2):
            attended = jnp.dot(
                expos[g].astype(BF16),
                values[q, :, g * HDIM : (g + 1) * HDIM],
                preferred_element_type=F32,
            )
            attended = (attended * factors[g]).astype(BF16)
            attended = jnp.concatenate(
                [attended[h * ROWS : (h + 1) * ROWS, :] for h in range(GROUP)], axis=1
            )
            own_att[m, g] = attended
            owns.append(attended)
            to_sibling_att(m, g).start()

        total = hbuf[m, :, pl.ds(pl.multiple_of(c * HALF, HALF), HALF)].astype(F32)
        for g in range(2):
            total = total + product(owns[g], w_out[g * G_W : (g + 1) * G_W, :])

        def third(j):
            cols = slice(j * CW, (j + 1) * CW)
            return total[:, cols] + product(sib_0, w_out[2 * G_W : 3 * G_W, cols])

        arrived(sib_att.at[m, 0], a_recv.at[m, 0])
        sib_0 = sib_att[m, 0]
        parts = [third(j) for j in range(EARLY)]
        arrived(sib_att.at[m, 1], a_recv.at[m, 1])
        sib_1 = sib_att[m, 1]
        for j in range(CHUNKS + 1):
            if j < CHUNKS:
                if j >= EARLY:
                    parts.append(third(j))
                cols = slice(j * CW, (j + 1) * CW)
                parts[j] = parts[j] + product(sib_1, w_out[3 * G_W :, cols])
            ready = 0 if j == 0 else j - 1
            if j != 1:
                stage[q, rows, ready * CW : (ready + 1) * CW] = parts[ready].astype(BF16)
                if not last:
                    to_next(m, ready).start()
        return carry

    def run(first, last):
        lax.fori_loop(0, COUNT, functools.partial(microbatch, first, last), 0)

    def settle(first, last, m, carry):
        for g in range(2):
            to_sibling_att(m, g).wait_send()
        for j in range(CHUNKS):
            if not last:
                to_next(m, j).wait_send()
            if not first:
                to_sibling_rows(m, j).wait_send()
        if first:
            for j in range(CHUNKS):
                spread(m // 2, lax.rem(m, 2), j, True).wait_send()
        return carry

    swap = pltpu.make_async_remote_copy(
        src_ref=stage.at[other], dst_ref=obuf,
        send_sem=o_send, recv_sem=o_recv,
        device_id=sibling, device_id_type=MESH,
    )

    @pl.when(s == 0)
    def _():
        run(True, False)

    @pl.when(jnp.logical_and(s > 0, s < SECTIONS - 1))
    def _():
        run(False, False)

    @pl.when(s == SECTIONS - 1)
    def _():
        run(False, True)

    def result(src, core, sem):
        cols = pl.ds(pl.multiple_of(core * HALF, HALF), HALF)
        return pltpu.make_async_copy(src, out_ref.at[0, :, cols], sem)

    swap.start()
    result(stage.at[c], c, local.at[0]).start()
    swap.wait_recv()
    result(obuf, other, local.at[1]).start()

    @pl.when(s == 0)
    def _():
        lax.fori_loop(0, COUNT, functools.partial(settle, True, False), 0)

    @pl.when(jnp.logical_and(s > 0, s < SECTIONS - 1))
    def _():
        lax.fori_loop(0, COUNT, functools.partial(settle, False, False), 0)

    @pl.when(s == SECTIONS - 1)
    def _():
        lax.fori_loop(0, COUNT, functools.partial(settle, False, True), 0)

    for mat in range(MATS):
        direct(mat, 4, other, sibling).wait_send()

        @pl.when(in_ring(mat))
        def _(mat=mat):
            for copy in directs(mat) + forwards(mat):
                copy.wait_send()

    for k in range(DETOURS):

        @pl.when(k < mine)
        def _(k=k):
            for core in (0, 1):
                lend(k, core).wait_send()

    def served_all(k, carry):
        for copy in lent_directs(k) + lent_forwards(k) + backs(k):
            copy.wait_send()
        return carry

    lax.fori_loop(serve_from, serve_to, served_all, 0)
    swap.wait_send()
    result(stage.at[c], c, local.at[0]).wait()
    result(obuf, other, local.at[1]).wait()


def on_device(inputs, gains, w_query, w_key, w_value, w_out):
    anywhere = pl.BlockSpec(memory_space=pl.ANY)
    vmem = pl.BlockSpec(memory_space=pltpu.VMEM)
    dma = pltpu.SemaphoreType.DMA
    return pl.pallas_call(
        kernel,
        out_shape=jax.ShapeDtypeStruct((1, SEQ, D), BF16),
        in_specs=[anywhere, vmem, anywhere, anywhere, anywhere, anywhere],
        out_specs=anywhere,
        scratch_shapes=[
            pltpu.VMEM((D, QKV_W), BF16),
            pltpu.VMEM((2 * Q_W, HALF), BF16),
            pltpu.VMEM((DETOURS, 8, PART, HALF), BF16),
            pltpu.VMEM((COUNT, ROWS, D), BF16),
            pltpu.VMEM((2, SEQ, HALF), BF16),
            pltpu.VMEM((COUNT, 2, ROWS, G_W), BF16),
            pltpu.VMEM((COUNT, 2, ROWS, G_W), BF16),
            pltpu.VMEM((2, SEQ, K_W), BF16),
            pltpu.VMEM((2, SEQ, K_W), BF16),
            pltpu.VMEM((SEQ, HALF), BF16),
            dma((8, MATS)),
            dma((MATS, 5)),
            dma((MATS, 2)),
            dma((DETOURS, 8)),
            dma((DETOURS, 2)),
            dma((DETOURS, 2, 2)),
            dma((DETOURS, 2)),
            dma((DETOURS, 6)),
            dma((COUNT, CHUNKS, 2)),
            dma((COUNT, CHUNKS)),
            dma((COUNT, CHUNKS)),
            dma((COUNT, 2)),
            dma((COUNT, 2)),
            dma(()),
            dma(()),
            dma((2,)),
        ],
        compiler_params=pltpu.CompilerParams(
            collective_id=0, has_side_effects=True, vmem_limit_bytes=56 * 2**20
        ),
    )(inputs, gains, w_query, w_key, w_value, w_out)


def solution(mesh):
    in_specs = (
        P("dp", None),
        P("section", None),
        P("section", "dp", None),
        P("section", "dp", None),
        P("section", "dp", None),
        P("section", "dp", None),
    )
    return jax.shard_map(
        on_device,
        mesh=mesh,
        in_specs=in_specs,
        out_specs=P("section", "dp", None),
        check_vma=False,
    )
```
